256 devices in a mesh: prow: 8 (over y, core), pcol: 32 (over x, z).
Axes of the slice: x: 4, y: 4, z: 8, core: 2. Of those that a mesh axis runs over, the one named last changes fastest.
Arguments:
- matrix_slab: float32 [2048, 4096], P('pcol', 'prow'), may hold values from -1024 to 1024
- contributions: float32 [8, 1024, 64, 256], P('prow', 'pcol'), may hold values from -3 to 3
- target_column: int32 [8, 1024], P('prow', 'pcol'), may hold values from 0 to 31, as said below
- target_rows: int32 [8, 1024], P('prow', 'pcol'), may hold values from 0 to 1
- live_rows: int32 [8, 1024], P('prow', 'pcol'), may hold values from 1 to 256
- pivot_index: int32 [1, 256], replicated, may hold values from 256 to 4095, as said below
Outputs:
- factored: float32 [2048, 4096], P('pcol', 'prow')
The draws below stay inside these ranges and needn't reach their ends.
Inputs may be any that keep to these rules, and one draw needn't show every extreme that they name: `pivot_index`: row k lists 256 distinct rows, each (k + 1) * 256 or more. `target_column`: of the 32 blocks held by one device, at most 2 have target column blocks within the columns of one index of pcol, and exactly 2 for some index.
All inputs are finite; a program needn't handle non-finite values.
Results may differ from the reference program's by a relative error of at most 0.0001.
Values sent between devices are 32-bit elements; how exact they have to be, the bound alone decides.
No kernel may reach another device: no remote copies, remote signals or barrier semaphores. Data moves between devices by JAX's collectives and lax.ppermute only.
A program may use at most 128 MiB of HBM per device.

```python
import jax
import jax.numpy as jnp
from jax import lax

SLAB = 2048
PW = 256
PANELS = 1
NB = 64
TR = 256
CB_DEV = 32
ROWS_DEV = 512
COLS_DEV = 64
ROWS = 4096
MOST = 2
CB_ALL = 1024
N_PROW = 8
N_PCOL = 32


def pivot_draw(key):
    pivot_list = []
    for panel_number in range(PANELS):
        offset = (panel_number + 1) * PW
        shuffled = jax.random.permutation(jax.random.fold_in(key, panel_number), ROWS - offset)
        pivot_list.append(shuffled[:PW] + offset)
    return jnp.stack(pivot_list).astype(jnp.int32)


def draw_pivot_index(key, part):
    return pivot_draw(jax.random.fold_in(key, 11))


def draw_matrix_slab(key, part):
    pivots = pivot_draw(jax.random.fold_in(key, 11))
    subkeys = jax.random.split(jax.random.fold_in(key, 23), 6)
    modest = jax.random.uniform(subkeys[0], (SLAB, ROWS), jnp.float32, -1.0, 1.0)
    strong = jax.random.uniform(subkeys[1], (SLAB, ROWS), jnp.float32, -1.0, 1.0) * PW
    initial = jnp.arange(ROWS, dtype=jnp.int32)
    already_used = jnp.zeros((ROWS,), jnp.bool_)
    pivot_marks = []
    holders = []
    for panel_number in range(PANELS):
        chosen = pivots[panel_number]
        source_rows = initial[chosen]
        already_used = already_used.at[source_rows].set(True)
        pivot_marks.append(already_used)
        holders.append(source_rows)
        panel_slots = jnp.arange(panel_number * PW, (panel_number + 1) * PW, dtype=jnp.int32)
        moved_out = initial[panel_slots]
        initial = initial.at[panel_slots].set(source_rows).at[chosen].set(moved_out)
    pivot_marks = jnp.stack(pivot_marks)
    column_panel = jnp.minimum(jnp.arange(SLAB) // PW, PANELS - 1)
    in_panels = (jnp.arange(SLAB) < PANELS * PW)[:, None]
    quiet_mask = jnp.logical_or(jnp.logical_not(in_panels), pivot_marks[column_panel])
    entries = jnp.where(quiet_mask, modest, strong)
    for panel_number in range(PANELS):
        panel_columns = panel_number * PW + jnp.arange(PW)
        block_entries = jax.random.uniform(jax.random.fold_in(subkeys[5], panel_number), (PW, PW), jnp.float32, -0.25 * PW, 0.25 * PW)
        entries = entries.at[panel_columns[:, None], holders[panel_number][None, :]].set(block_entries)
        sign_flip = jnp.where(jax.random.bernoulli(jax.random.fold_in(subkeys[2], panel_number), 0.5, (PW,)), 1.0, -1.0)
        magnitude = jax.random.uniform(jax.random.fold_in(subkeys[3], panel_number), (PW,), jnp.float32, 3.0 * PW, 4.0 * PW)
        entries = entries.at[panel_columns, holders[panel_number]].set(sign_flip * magnitude)
    return entries


def draw_target_column(key, part):
    local_blocks = COLS_DEV // NB

    def one_device(device_key):
        first_key, second_key, third_key, fourth_key = jax.random.split(device_key, 4)
        slot_owner = jnp.arange(N_PCOL * MOST, dtype=jnp.int32) // MOST
        busiest = jax.random.randint(first_key, (), 0, N_PCOL)
        others = jax.random.permutation(second_key, N_PCOL * MOST - MOST)[:CB_DEV - MOST] + MOST
        picked = jnp.concatenate([jnp.arange(MOST, dtype=jnp.int32), others.astype(jnp.int32)])
        owners = (slot_owner[picked] + busiest) % N_PCOL
        owners = owners[jax.random.permutation(third_key, CB_DEV)]
        within = jax.random.randint(fourth_key, (CB_DEV,), 0, local_blocks)
        return owners * local_blocks + within
    device_keys = jax.random.split(jax.random.fold_in(key, 31), N_PROW * N_PCOL)
    return jax.vmap(one_device)(device_keys).reshape(N_PROW, N_PCOL * CB_DEV).astype(jnp.int32)


def set_ends(values, own_key, low, high):
    longest = values.shape.index(max(values.shape))
    spots = []
    for shift in (0, 1):
        where = [jax.random.randint(jax.random.fold_in(own_key, axis), (), 0, length) for axis, length in enumerate(values.shape)]
        where[longest] = (where[longest] + shift) % values.shape[longest]
        spots.append(tuple(where))
    return values.at[spots[0]].set(low).at[spots[1]].set(high)


def shard_levels(key, shape, shards, low, largest):
    def one(dim, blocks):
        draws = jax.random.uniform(jax.random.fold_in(jax.random.fold_in(key, 6), dim), (blocks,), jnp.float32, low / len(shards), largest / len(shards))
        return jnp.repeat(jnp.exp(draws), shape[dim] // blocks).reshape((-1,) + (1,) * (len(shape) - dim - 1))

    level = one(*shards[0])
    for cut in shards[1:]:
        level = level * one(*cut)
    return level


def scatter_about(own_key, shape, scale, limit, cuts=(), kind=jnp.bfloat16):
    level = shard_levels(own_key, shape, cuts, -0.22, 0.18) if cuts else 1.0
    values = jax.random.normal(own_key, shape, jnp.float32) * scale * level
    return jnp.minimum(jnp.maximum(values, -limit), limit).astype(kind)


def setup_inputs(seed: int = 0) -> dict:
    keys = jax.random.split(jax.random.key(seed), 7)
    return {
        "matrix_slab": draw_matrix_slab(jax.random.fold_in(keys[6], 71), 0),
        "contributions": scatter_about(keys[1], (N_PROW, CB_ALL, NB, TR), 0.5, 3.0, ((0, 8), (1, 32)), jnp.float32),
        "target_column": draw_target_column(jax.random.fold_in(keys[6], 71), 0),
        "target_rows": set_ends(jax.random.randint(keys[3], (N_PROW, CB_ALL), 0, ROWS_DEV // TR), jax.random.fold_in(keys[3], 1), 0, (ROWS_DEV // TR) - 1).astype(jnp.int32),
        "live_rows": set_ends(jax.random.randint(keys[4], (N_PROW, CB_ALL), 1, TR + 1), jax.random.fold_in(keys[4], 1), 1, TR).astype(jnp.int32),
        "pivot_index": draw_pivot_index(jax.random.fold_in(keys[6], 71), 0),
    }


HIGHEST = lax.Precision.HIGHEST

def factor_block(square):
    extent = square.shape[0]
    if extent <= 16:
        for column in range(extent - 1):
            ratios = square[column + 1:, column] / square[column, column]
            square = square.at[column + 1:, column].set(ratios)
            square = square.at[column + 1:, column + 1:].add(-ratios[:, None] * square[column, column + 1:][None, :])
        return square
    middle = extent // 2
    top_left = factor_block(square[:middle, :middle])
    lower_unit = jnp.tril(top_left, -1) + jnp.eye(middle, dtype=square.dtype)
    upper_part = jnp.triu(top_left)
    right_part = jax.scipy.linalg.solve_triangular(lower_unit, square[:middle, middle:], lower=True, unit_diagonal=True)
    left_part = jax.scipy.linalg.solve_triangular(upper_part.T, square[middle:, :middle].T, lower=True).T
    schur_part = square[middle:, middle:] - jnp.dot(left_part, right_part, precision=HIGHEST)
    bottom = factor_block(schur_part)
    upper_half = jnp.concatenate([top_left, right_part], axis=1)
    lower_half = jnp.concatenate([left_part, bottom], axis=1)
    return jnp.concatenate([upper_half, lower_half], axis=0)

def split_factors(packed):
    extent = packed.shape[0]
    lower_unit = jnp.tril(packed, -1) + jnp.eye(extent, dtype=packed.dtype)
    return (lower_unit, jnp.triu(packed))

def reference(matrix_slab, contributions, target_column, target_rows, live_rows, pivot_index):
    blocks = contributions.reshape(N_PROW * CB_ALL, NB, TR)
    lengths = live_rows.reshape(-1)
    column_anchor = (target_column.reshape(-1) * NB).astype(jnp.int32)
    row_anchor = (jnp.arange(N_PROW, dtype=jnp.int32)[:, None] * ROWS_DEV + target_rows * TR).reshape(-1).astype(jnp.int32)
    positions = jnp.arange(TR, dtype=jnp.int32)

    def add_block(index, current):
        single = blocks[index] * (positions < lengths[index]).astype(blocks.dtype)[None, :]
        anchor = (column_anchor[index], row_anchor[index])
        window = lax.dynamic_slice(current, anchor, (NB, TR))
        return lax.dynamic_update_slice(current, window + single, anchor)
    matrix = lax.fori_loop(0, N_PROW * CB_ALL, add_block, matrix_slab)
    rows_all = jnp.arange(ROWS, dtype=jnp.int32)
    for panel_number in range(PANELS):
        panel_start = panel_number * PW
        panel_end = panel_start + PW
        chosen = pivot_index[panel_number]
        displaced = matrix[:, panel_start:panel_end]
        incoming = matrix[:, chosen]
        matrix = matrix.at[:, chosen].set(displaced)
        matrix = matrix.at[:, panel_start:panel_end].set(incoming)
        panel_cols = matrix[panel_start:panel_end, :]
        packed = factor_block(panel_cols[:, panel_start:panel_end].T)
        lower_unit, upper_part = split_factors(packed)
        lower_cols = jax.scipy.linalg.solve_triangular(upper_part.T, panel_cols, lower=True)
        upper_rows = jax.scipy.linalg.solve_triangular(lower_unit, matrix[:, panel_start:panel_end].T, lower=True, unit_diagonal=True)
        below_rows = rows_all >= panel_end
        renewed = panel_cols.at[:, panel_start:panel_end].set(packed.T)
        renewed = jnp.where(below_rows[None, :], lower_cols, renewed)
        trailing = upper_rows[:, panel_end:].T
        update = jnp.dot(trailing, lower_cols[:, panel_end:], precision=HIGHEST)
        matrix = matrix.at[panel_start:panel_end, :].set(renewed)
        matrix = matrix.at[panel_end:, panel_start:panel_end].set(trailing)
        matrix = matrix.at[panel_end:, panel_end:].add(-update)
    return matrix
```

```python
import functools

import jax
import jax.numpy as jnp
from jax import lax
from jax.experimental import pallas as pl
from jax.experimental.pallas import tpu as pltpu
from jax.sharding import Mesh
from jax.sharding import PartitionSpec as P

SLAB = 2048
PW = 256
NB = 64
TR = 256
CB_DEV = 32
NX = 4
NZ = 8
PROW = 8
OWNERS = PW // NB
ROWS_DEV = 512
G = 8
AX, AZ, AY = "pcol_0", "pcol_1", "prow"
PCOL = (AX, AZ)
HIGHEST = lax.Precision.HIGHEST
F32 = jnp.float32
MIB = 1024 * 1024
VMEM = pl.BlockSpec(memory_space=pltpu.VMEM)
SMEM = pl.BlockSpec(memory_space=pltpu.SMEM)
HBM = pl.BlockSpec(memory_space=pltpu.HBM)


def dotf(a, b):
    return jnp.dot(a, b, precision=HIGHEST, preferred_element_type=F32)


def dot_nt(a, b):
    dims = (((1,), (1,)), ((), ()))
    return lax.dot_general(a, b, dims, precision=HIGHEST, preferred_element_type=F32)


CH = 8


def scatter_kernel(tc_ref, tr_ref, lr_ref, blocks_ref, slab_ref, pan_out, dense_out, *scratch):
    tc, tr, lr, own, buf, dense, pan, in_sem, num_sem, out_sem = scratch
    my_x = lax.axis_index(AX)
    my_z = lax.axis_index(AZ)
    owner = (my_x == 0) & (my_z < OWNERS)
    numbers = [
        pltpu.make_async_copy(src, dst, num_sem.at[i])
        for i, (src, dst) in enumerate(((tc_ref, tc), (tr_ref, tr), (lr_ref, lr), (slab_ref, own)))
    ]
    for number in numbers:
        number.start()
    loads = [
        pltpu.make_async_copy(blocks_ref.at[pl.ds(i * CH, CH)], buf.at[pl.ds(i * CH, CH)], in_sem.at[i])
        for i in range(CB_DEV // CH)
    ]
    for load in loads:
        load.start()

    def clear(i, carry):
        dense[i] = jnp.zeros((NB, ROWS_DEV), F32)
        return carry

    lax.fori_loop(0, NX * NZ, clear, 0)
    for number in numbers:
        number.wait()
    for i in range(OWNERS):
        pan[i] = jnp.where(owner & (my_z == i), own[...], 0.0)
    lane = lax.broadcasted_iota(jnp.int32, (NB, TR), 1)

    def add(i, carry):
        col = tc[0, i]
        at = pl.ds(pl.multiple_of(tr[0, i] * TR, TR), TR)
        block = jnp.where(lane < lr[0, i], buf[i], 0.0)

        @pl.when(col < OWNERS)
        def _():
            pan[col, :, at] = pan[col, :, at] + block

        @pl.when(col >= OWNERS)
        def _():
            slot = (col % NZ) * NX + (col // NZ + NX - my_x) % NX
            dense[slot, :, at] = dense[slot, :, at] + block

        return carry

    for i in range(CB_DEV // CH):
        loads[i].wait()
        lax.fori_loop(i * CH, (i + 1) * CH, add, 0)
    stores = [
        pltpu.make_async_copy(pan, pan_out, out_sem.at[0]),
        pltpu.make_async_copy(dense, dense_out, out_sem.at[1]),
    ]
    for store in stores:
        store.start()
    for store in stores:
        store.wait()


def scatter(tc, tr, lr, blocks, slab):
    return pl.pallas_call(
        scatter_kernel,
        out_shape=[
            jax.ShapeDtypeStruct((OWNERS, NB, ROWS_DEV), F32),
            jax.ShapeDtypeStruct((NX * NZ, NB, ROWS_DEV), F32),
        ],
        in_specs=[HBM] * 5,
        out_specs=[HBM] * 2,
        scratch_shapes=[pltpu.SMEM((1, CB_DEV), jnp.int32)] * 3
        + [
            pltpu.VMEM((NB, ROWS_DEV), F32),
            pltpu.VMEM((CB_DEV, NB, TR), F32),
            pltpu.VMEM((NX * NZ, NB, ROWS_DEV), F32),
            pltpu.VMEM((OWNERS, NB, ROWS_DEV), F32),
            pltpu.SemaphoreType.DMA((CB_DEV // CH,)),
            pltpu.SemaphoreType.DMA((4,)),
            pltpu.SemaphoreType.DMA((2,)),
        ],
        compiler_params=pltpu.CompilerParams(vmem_limit_bytes=56 * MIB),
        name="scatter",
    )(tc, tr, lr, blocks, slab)


def shift(value, axis, n, step):
    return lax.ppermute(value, axis, [(i, (i + step) % n) for i in range(n)])


def ring_sum(rel, halves, axis, n):
    h = halves[0].shape[0]
    ahead = shift(halves[0], axis, n, 1)
    back = shift(halves[1], axis, n, -1)
    for d in range(n // 2 - 1, 0, -1):
        up, down = rel[d], rel[n - d]
        if ahead.shape[0] == h and d == n // 2 - 1:
            up = jnp.concatenate([up[:h] + ahead, up[h:]], axis=0)
            down = jnp.concatenate([down[:h], down[h:] + back], axis=0)
        else:
            up, down = up + ahead, down + back
        ahead = shift(up, axis, n, 1)
        back = shift(down, axis, n, -1)
    return rel[0] + ahead + back


def sum_along_z(dense):
    return lax.psum_scatter(dense.reshape(NZ, NX, NB, ROWS_DEV), AZ, scatter_dimension=0, tiled=True)[0]


def sum_along_x(part):
    rows = [part[i] for i in range(NX)]
    half = rows[NX // 2]
    return ring_sum(rows, (half[: NB // 2], half[NB // 2 :]), AX, NX)


def exchange(value, axis):
    return lax.all_to_all(value, axis, split_axis=0, concat_axis=0, tiled=True)


def gather(value, axis, n):
    copies = jnp.broadcast_to(value, (n, *value.shape))
    return exchange(copies, axis)


def factor_kernel(t_ref, packed_ref, loinv_ref, upinv_ref, x_ref, v_ref, r_ref, lo_ref, ti_ref, b_ref):
    x_ref[...] = t_ref[...]
    b_ref[...] = jnp.zeros_like(b_ref)
    ti_ref[...] = jnp.zeros_like(ti_ref)
    lo_ref[...] = jnp.zeros_like(lo_ref)
    r_ref[...] = jnp.zeros_like(r_ref)
    lane = lax.broadcasted_iota(jnp.int32, (G, PW), 1)
    row8 = lax.broadcasted_iota(jnp.int32, (G, 128), 0)
    row = lax.broadcasted_iota(jnp.int32, (G, PW), 0)
    lane1 = lax.broadcasted_iota(jnp.int32, (1, PW), 1)
    panel = t_ref[0:G, :]
    steps = PW // G
    for b in range(steps):
        k0 = G * b
        inblk = (lane >= k0) & (lane < k0 + G)
        cols = [jnp.broadcast_to(panel[:, k0 + j : k0 + j + 1], (G, 128)) for j in range(G)]
        nxt = None
        if b + 1 < steps:
            below = x_ref[k0 + G : k0 + 2 * G, :]
            mult = [jnp.broadcast_to(below[:, k0 + j : k0 + j + 1], (G, PW)) for j in range(G)]
            nxt = jnp.where(inblk, 0.0, below)
        lo_block = jnp.zeros((G, PW), F32)
        for k in range(G):
            ck = cols[k]
            inv = 1.0 / jnp.broadcast_to(ck[k : k + 1, :], (G, 128))
            inv2 = jnp.concatenate([inv, inv], axis=1)
            ck2 = jnp.concatenate([ck, ck], axis=1)
            for j in range(k + 1, G):
                m = jnp.broadcast_to(cols[j][k : k + 1, :], (G, 128)) * inv
                cols[j] = jnp.where(row8 == k, m, cols[j] - ck * m)
            lo_block = jnp.where((lane == k0 + k) & (row >= k), ck2, lo_block)
            panel = jnp.where(lane == k0 + k, jnp.where(row == k, 1.0, 0.0), panel)
            scaled = jnp.broadcast_to(panel[k : k + 1, :], (G, PW)) * inv2
            v_ref[k0 + k : k0 + k + 1, :] = scaled[0:1]
            panel = jnp.where(row == k, scaled, panel - ck2 * scaled)
        lo_ref[k0 : k0 + G, :] = lo_block
        ti_ref[k0 : k0 + G, :] = jnp.where(inblk, panel, 0.0)
        if nxt is not None:
            for j in range(G):
                nxt = nxt - mult[j] * jnp.broadcast_to(panel[j : j + 1, :], (G, PW))
        tile = (k0 // 128) * 128
        kk = k0 % 128
        slot = b % 2
        if b >= 2:
            old = (k0 - 2 * G) % 128
            b_ref[slot, old : old + G, :] = jnp.zeros((G, PW), F32)
        b_ref[slot, kk : kk + G, :] = panel
        inb = (lane1 >= k0) & (lane1 < k0 + G)
        raw = x_ref[:, tile : tile + 128]
        r_ref[:, tile : tile + 128] = jnp.where(inb[:, tile : tile + 128], raw, r_ref[:, tile : tile + 128])
        if b + 1 < steps:
            x_ref[...] = jnp.where(inb, 0.0, x_ref[...]) - dotf(raw, b_ref[slot])
            x_ref[k0 : k0 + G, :] = -panel
        unit = jnp.where(row == lane - k0, 1.0, 0.0)
        r_ref[k0 : k0 + G, :] = jnp.where(inblk, unit, r_ref[k0 : k0 + G, :])
        panel = nxt
    z = dotf(r_ref[...], dotf(ti_ref[...], lo_ref[...]))
    v = v_ref[...]
    rr = lax.broadcasted_iota(jnp.int32, (PW, PW), 0)
    cc = lax.broadcasted_iota(jnp.int32, (PW, PW), 1)
    same = (rr // G) == (cc // G)
    packed_ref[...] = jnp.where(rr < cc, v, jnp.where(same, lo_ref[...], z))
    loinv_ref[...] = jnp.where(rr >= cc, v, 0.0)
    upinv_ref[...] = jnp.where(rr < cc, z, jnp.where(rr == cc, 1.0, 0.0))


def factor(t):
    return pl.pallas_call(
        factor_kernel,
        out_shape=[jax.ShapeDtypeStruct((PW, PW), F32)] * 3,
        in_specs=[VMEM],
        out_specs=[VMEM] * 3,
        scratch_shapes=[pltpu.VMEM((PW, PW), F32)] * 5 + [pltpu.VMEM((2, 128, PW), F32)],
        compiler_params=pltpu.CompilerParams(vmem_limit_bytes=16 * MIB),
        cost_estimate=pl.CostEstimate(flops=40_000_000, bytes_accessed=60_000_000, transcendentals=0),
        name="factor",
    )(t)


def finish_kernel(pivot_ref, matrix_ref, offers_ref, panel_ref, packed_ref, loinv_ref, upinv_ref, out_ref, low_ref):
    row_group = lax.axis_index(AY)
    col_group = lax.axis_index(AX) * NZ + lax.axis_index(AZ)
    rows = lax.broadcasted_iota(jnp.int32, (PW, ROWS_DEV), 1) + row_group * ROWS_DEV
    pick = jnp.where(pivot_ref[...] == rows, 1.0, 0.0)
    hit = jnp.sum(pick, axis=0, keepdims=True) > 0.0
    low_ref[...] = dotf(loinv_ref[...], panel_ref[...])
    matrix = jnp.where(hit, dotf(offers_ref[0, :, PW:], pick), matrix_ref[...])
    inc = offers_ref[0, :, :PW]
    for i in range(1, PROW):
        inc = inc + offers_ref[i, :, :PW]
    upper = dotf(inc, upinv_ref[...])
    out_ref[...] = matrix - dotf(upper, low_ref[...])

    @pl.when(row_group == 0)
    def _():
        out_ref[:, :PW] = upper

    @pl.when(col_group < OWNERS)
    def _():
        at = pl.ds(pl.multiple_of(col_group * NB, NB), NB)
        out_ref[...] = low_ref[at, :]

        @pl.when(row_group == 0)
        def _():
            out_ref[:, :PW] = packed_ref[at, :]


def finish(pivot, matrix, offers, panel, packed, loinv, upinv):
    return pl.pallas_call(
        finish_kernel,
        out_shape=jax.ShapeDtypeStruct((NB, ROWS_DEV), F32),
        in_specs=[VMEM] * 7,
        out_specs=VMEM,
        scratch_shapes=[pltpu.VMEM((PW, ROWS_DEV), F32)],
        compiler_params=pltpu.CompilerParams(vmem_limit_bytes=16 * MIB),
        name="finish",
    )(pivot, matrix, offers, panel, packed, loinv, upinv)


def per_device(matrix_slab, contributions, target_column, target_rows, live_rows, pivot_index):
    row_group = lax.axis_index(AY)
    pan, dense = scatter(target_column, target_rows, live_rows, contributions[0], matrix_slab)
    pivot = pivot_index[0]
    pick = (pivot[:, None] == row_group * ROWS_DEV + jnp.arange(ROWS_DEV)[None, :]).astype(F32)
    hit = jnp.sum(pick, axis=0) > 0

    with jax.named_scope("panel_sum"):
        chunk = exchange(pan, AX).sum(axis=0)
        chunk = exchange(chunk.reshape(NZ, NB // NZ, ROWS_DEV), AZ).sum(axis=0)
    with jax.named_scope("panel_swap"):
        offer = jnp.concatenate([dot_nt(chunk, pick), chunk[:, :PW]], axis=1)
        offers = gather(offer, AY, PROW)
        diag = offers[:, :, :PW].sum(axis=0)
        moved = offers[0, :, PW:]
        chunk = jnp.where(hit[None, :], dotf(moved, pick), chunk)
    with jax.named_scope("slab_sum"):
        part = sum_along_z(dense)
    with jax.named_scope("panel_gather"):
        both = jnp.concatenate([diag, chunk], axis=1)
        both = gather(both, AZ, NZ).reshape(NB, PW + ROWS_DEV)
        both = gather(both, AX, NX).reshape(PW, PW + ROWS_DEV)
        both, part = lax.optimization_barrier((both, part))
    with jax.named_scope("slab_sum"):
        matrix = matrix_slab + sum_along_x(part)
    with jax.named_scope("slab_swap"):
        offer = jnp.concatenate([dot_nt(matrix, pick), matrix[:, :PW]], axis=1)
        diag = lax.optimization_barrier((both[:, :PW], offer))[0]
        offers = gather(offer, AY, PROW)
    packed, loinv, upinv = factor(diag)
    return finish(pivot[:, None], matrix, offers, both[:, PW:], packed, loinv, upinv)


def solution(mesh):
    torus = Mesh(mesh.devices.reshape(mesh.shape["prow"], NX, NZ), (AY, AX, AZ))
    placed = (
        P(PCOL, AY),
        P(AY, PCOL, None, None),
        P(AY, PCOL),
        P(AY, PCOL),
        P(AY, PCOL),
        P(),
    )
    return jax.shard_map(
        per_device, mesh=torus, in_specs=placed, out_specs=P(PCOL, AY), check_vma=False
    )
```

```python
import functools

import jax
import jax.numpy as jnp
from jax import lax
from jax.experimental import pallas as pl
from jax.experimental.pallas import tpu as pltpu
from jax.sharding import Mesh
from jax.sharding import PartitionSpec as P

SLAB = 2048
PW = 256
NB = 64
TR = 256
CB_DEV = 32
NX = 4
NZ = 8
PROW = 8
OWNERS = PW // NB
ROWS_DEV = 512
G = 8
AX, AZ, AY = "pcol_0", "pcol_1", "prow"
PCOL = (AX, AZ)
HIGHEST = lax.Precision.HIGHEST
F32 = jnp.float32
MIB = 1024 * 1024
VMEM = pl.BlockSpec(memory_space=pltpu.VMEM)
SMEM = pl.BlockSpec(memory_space=pltpu.SMEM)
HBM = pl.BlockSpec(memory_space=pltpu.HBM)


def dotf(a, b):
    return jnp.dot(a, b, precision=HIGHEST, preferred_element_type=F32)


def dot_nt(a, b):
    dims = (((1,), (1,)), ((), ()))
    return lax.dot_general(a, b, dims, precision=HIGHEST, preferred_element_type=F32)


CH = 8


def scatter_kernel(tc_ref, tr_ref, lr_ref, blocks_ref, slab_ref, pan_out, *rest):
    dense_outs = rest[:9]
    tc, tr, lr, own, buf, dense, pan, in_sem, num_sem, out_sem = rest[9:]
    my_x = lax.axis_index(AX)
    my_z = lax.axis_index(AZ)
    owner = (my_x == 0) & (my_z < OWNERS)
    numbers = [
        pltpu.make_async_copy(src, dst, num_sem.at[i])
        for i, (src, dst) in enumerate(((tc_ref, tc), (tr_ref, tr), (lr_ref, lr), (slab_ref, own)))
    ]
    for number in numbers:
        number.start()
    loads = [
        pltpu.make_async_copy(blocks_ref.at[pl.ds(i * CH, CH)], buf.at[pl.ds(i * CH, CH)], in_sem.at[i])
        for i in range(CB_DEV // CH)
    ]
    for load in loads:
        load.start()

    def clear(i, carry):
        dense[i] = jnp.zeros((NB, ROWS_DEV), F32)
        return carry

    lax.fori_loop(0, NX * NZ, clear, 0)
    for number in numbers:
        number.wait()
    for i in range(OWNERS):
        pan[i] = jnp.where(owner & (my_z == i), own[...], 0.0)
    lane = lax.broadcasted_iota(jnp.int32, (NB, TR), 1)

    def add(i, carry):
        col = tc[0, i]
        at = pl.ds(pl.multiple_of(tr[0, i] * TR, TR), TR)
        block = jnp.where(lane < lr[0, i], buf[i], 0.0)

        @pl.when(col < OWNERS)
        def _():
            pan[col, :, at] = pan[col, :, at] + block

        @pl.when(col >= OWNERS)
        def _():
            slot = ((col % NZ + NZ - my_z) % NZ) * NX + (col // NZ + NX - my_x) % NX
            dense[slot, :, at] = dense[slot, :, at] + block

        return carry

    for i in range(CB_DEV // CH):
        loads[i].wait()
        lax.fori_loop(i * CH, (i + 1) * CH, add, 0)
    stores = [pltpu.make_async_copy(pan, pan_out, out_sem.at[0])]
    base = 0
    for i, out in enumerate(dense_outs):
        stores.append(pltpu.make_async_copy(dense.at[pl.ds(base, out.shape[0])], out, out_sem.at[1 + i]))
        base += out.shape[0]
    for store in stores:
        store.start()
    for store in stores:
        store.wait()


def scatter(tc, tr, lr, blocks, slab):
    sizes = [NX] * 4 + [NX // 2] * 2 + [NX] * 3
    outs = pl.pallas_call(
        scatter_kernel,
        out_shape=[jax.ShapeDtypeStruct((n, NB, ROWS_DEV), F32) for n in [OWNERS] + sizes],
        in_specs=[HBM] * 5,
        out_specs=[HBM] * 10,
        scratch_shapes=[pltpu.SMEM((1, CB_DEV), jnp.int32)] * 3
        + [
            pltpu.VMEM((NB, ROWS_DEV), F32),
            pltpu.VMEM((CB_DEV, NB, TR), F32),
            pltpu.VMEM((NX * NZ, NB, ROWS_DEV), F32),
            pltpu.VMEM((OWNERS, NB, ROWS_DEV), F32),
            pltpu.SemaphoreType.DMA((CB_DEV // CH,)),
            pltpu.SemaphoreType.DMA((4,)),
            pltpu.SemaphoreType.DMA((10,)),
        ],
        compiler_params=pltpu.CompilerParams(vmem_limit_bytes=56 * MIB),
        name="scatter",
    )(tc, tr, lr, blocks, slab)
    return outs[0], list(outs[1:])


def shift(value, axis, n, step):
    return lax.ppermute(value, axis, [(i, (i + step) % n) for i in range(n)])


def ring_sum(rel, halves, axis, n):
    h = halves[0].shape[0]
    pair = yield shift(halves[0], axis, n, 1), shift(halves[1], axis, n, -1)
    for d in range(n // 2 - 1, 0, -1):
        up, down = rel[d], rel[n - d]
        if d == n // 2 - 1:
            up = jnp.concatenate([up[:h] + pair[0], up[h:]], axis=0)
            down = jnp.concatenate([down[:h], down[h:] + pair[1]], axis=0)
        else:
            up, down = up + pair[0], down + pair[1]
        pair = yield shift(up, axis, n, 1), shift(down, axis, n, -1)
    yield rel[0] + pair[0] + pair[1]


def tied(value, pair):
    value, first, second = lax.optimization_barrier((value, *pair))
    return value, (first, second)


def exchange(value, axis):
    return lax.all_to_all(value, axis, split_axis=0, concat_axis=0, tiled=True)


def gather(value, axis, n):
    copies = jnp.broadcast_to(value, (n, *value.shape))
    return exchange(copies, axis)


def factor_kernel(t_ref, packed_ref, loinv_ref, upinv_ref, x_ref, v_ref, r_ref, lo_ref, ti_ref, b_ref):
    x_ref[...] = t_ref[...]
    b_ref[...] = jnp.zeros_like(b_ref)
    ti_ref[...] = jnp.zeros_like(ti_ref)
    lo_ref[...] = jnp.zeros_like(lo_ref)
    r_ref[...] = jnp.zeros_like(r_ref)
    lane = lax.broadcasted_iota(jnp.int32, (G, PW), 1)
    row8 = lax.broadcasted_iota(jnp.int32, (G, 128), 0)
    row = lax.broadcasted_iota(jnp.int32, (G, PW), 0)
    lane1 = lax.broadcasted_iota(jnp.int32, (1, PW), 1)
    panel = t_ref[0:G, :]
    steps = PW // G
    for b in range(steps):
        k0 = G * b
        inblk = (lane >= k0) & (lane < k0 + G)
        cols = [jnp.broadcast_to(panel[:, k0 + j : k0 + j + 1], (G, 128)) for j in range(G)]
        nxt = None
        if b + 1 < steps:
            below = x_ref[k0 + G : k0 + 2 * G, :]
            mult = [jnp.broadcast_to(below[:, k0 + j : k0 + j + 1], (G, PW)) for j in range(G)]
            nxt = jnp.where(inblk, 0.0, below)
        lo_block = jnp.zeros((G, PW), F32)
        for k in range(G):
            ck = cols[k]
            inv = 1.0 / jnp.broadcast_to(ck[k : k + 1, :], (G, 128))
            inv2 = jnp.concatenate([inv, inv], axis=1)
            ck2 = jnp.concatenate([ck, ck], axis=1)
            for j in range(k + 1, G):
                m = jnp.broadcast_to(cols[j][k : k + 1, :], (G, 128)) * inv
                cols[j] = jnp.where(row8 == k, m, cols[j] - ck * m)
            lo_block = jnp.where((lane == k0 + k) & (row >= k), ck2, lo_block)
            panel = jnp.where(lane == k0 + k, jnp.where(row == k, 1.0, 0.0), panel)
            scaled = jnp.broadcast_to(panel[k : k + 1, :], (G, PW)) * inv2
            v_ref[k0 + k : k0 + k + 1, :] = scaled[0:1]
            panel = jnp.where(row == k, scaled, panel - ck2 * scaled)
        lo_ref[k0 : k0 + G, :] = lo_block
        ti_ref[k0 : k0 + G, :] = jnp.where(inblk, panel, 0.0)
        if nxt is not None:
            for j in range(G):
                nxt = nxt - mult[j] * jnp.broadcast_to(panel[j : j + 1, :], (G, PW))
        tile = (k0 // 128) * 128
        kk = k0 % 128
        slot = b % 2
        if b >= 2:
            old = (k0 - 2 * G) % 128
            b_ref[slot, old : old + G, :] = jnp.zeros((G, PW), F32)
        b_ref[slot, kk : kk + G, :] = panel
        inb = (lane1 >= k0) & (lane1 < k0 + G)
        raw = x_ref[:, tile : tile + 128]
        r_ref[:, tile : tile + 128] = jnp.where(inb[:, tile : tile + 128], raw, r_ref[:, tile : tile + 128])
        if b + 1 < steps:
            x_ref[...] = jnp.where(inb, 0.0, x_ref[...]) - dotf(raw, b_ref[slot])
            x_ref[k0 : k0 + G, :] = -panel
        unit = jnp.where(row == lane - k0, 1.0, 0.0)
        r_ref[k0 : k0 + G, :] = jnp.where(inblk, unit, r_ref[k0 : k0 + G, :])
        panel = nxt
    z = dotf(r_ref[...], dotf(ti_ref[...], lo_ref[...]))
    v = v_ref[...]
    rr = lax.broadcasted_iota(jnp.int32, (PW, PW), 0)
    cc = lax.broadcasted_iota(jnp.int32, (PW, PW), 1)
    same = (rr // G) == (cc // G)
    packed_ref[...] = jnp.where(rr < cc, v, jnp.where(same, lo_ref[...], z))
    loinv_ref[...] = jnp.where(rr >= cc, v, 0.0)
    upinv_ref[...] = jnp.where(rr < cc, z, jnp.where(rr == cc, 1.0, 0.0))


def factor(t):
    return pl.pallas_call(
        factor_kernel,
        out_shape=[jax.ShapeDtypeStruct((PW, PW), F32)] * 3,
        in_specs=[VMEM],
        out_specs=[VMEM] * 3,
        scratch_shapes=[pltpu.VMEM((PW, PW), F32)] * 5 + [pltpu.VMEM((2, 128, PW), F32)],
        compiler_params=pltpu.CompilerParams(vmem_limit_bytes=16 * MIB),
        cost_estimate=pl.CostEstimate(flops=40_000_000, bytes_accessed=60_000_000, transcendentals=0),
        name="factor",
    )(t)


def finish_kernel(pivot_ref, matrix_ref, offers_ref, panel_ref, packed_ref, loinv_ref, upinv_ref, out_ref, low_ref):
    row_group = lax.axis_index(AY)
    col_group = lax.axis_index(AX) * NZ + lax.axis_index(AZ)
    rows = lax.broadcasted_iota(jnp.int32, (PW, ROWS_DEV), 1) + row_group * ROWS_DEV
    pick = jnp.where(pivot_ref[...] == rows, 1.0, 0.0)
    hit = jnp.sum(pick, axis=0, keepdims=True) > 0.0
    low_ref[...] = dotf(loinv_ref[...], panel_ref[...])
    matrix = jnp.where(hit, dotf(offers_ref[0, :, PW:], pick), matrix_ref[...])
    inc = offers_ref[0, :, :PW]
    for i in range(1, PROW):
        inc = inc + offers_ref[i, :, :PW]
    upper = dotf(inc, upinv_ref[...])
    out_ref[...] = matrix - dotf(upper, low_ref[...])

    @pl.when(row_group == 0)
    def _():
        out_ref[:, :PW] = upper

    @pl.when(col_group < OWNERS)
    def _():
        at = pl.ds(pl.multiple_of(col_group * NB, NB), NB)
        out_ref[...] = low_ref[at, :]

        @pl.when(row_group == 0)
        def _():
            out_ref[:, :PW] = packed_ref[at, :]


def finish(pivot, matrix, offers, panel, packed, loinv, upinv):
    return pl.pallas_call(
        finish_kernel,
        out_shape=jax.ShapeDtypeStruct((NB, ROWS_DEV), F32),
        in_specs=[VMEM] * 7,
        out_specs=VMEM,
        scratch_shapes=[pltpu.VMEM((PW, ROWS_DEV), F32)],
        compiler_params=pltpu.CompilerParams(vmem_limit_bytes=16 * MIB),
        name="finish",
    )(pivot, matrix, offers, panel, packed, loinv, upinv)


def per_device(matrix_slab, contributions, target_column, target_rows, live_rows, pivot_index):
    row_group = lax.axis_index(AY)
    pan, dense = scatter(target_column, target_rows, live_rows, contributions[0], matrix_slab)
    pivot = pivot_index[0]
    pick = (pivot[:, None] == row_group * ROWS_DEV + jnp.arange(ROWS_DEV)[None, :]).astype(F32)
    hit = jnp.sum(pick, axis=0) > 0

    along_z = ring_sum(dense[:4] + [None] + dense[6:], (dense[4], dense[5]), AZ, NZ)
    pair = next(along_z)
    chunk, pair = tied(exchange(pan, AX), pair)
    pair = along_z.send(pair)
    chunk = exchange(chunk.sum(axis=0).reshape(NZ, NB // NZ, ROWS_DEV), AZ)
    chunk, pair = tied(chunk, pair)
    pair = along_z.send(pair)
    chunk = chunk.sum(axis=0)
    offer = jnp.concatenate([dot_nt(chunk, pick), chunk[:, :PW]], axis=1)
    offers, pair = tied(gather(offer, AY, PROW), pair)
    pair = along_z.send(pair)
    moved = offers[0, :, PW:]
    chunk = jnp.where(hit[None, :], dotf(moved, pick), chunk)
    both = jnp.concatenate([offers[:, :, :PW].sum(axis=0), chunk], axis=1)
    both, pair = tied(gather(both, AZ, NZ), pair)
    part = along_z.send(pair)
    half = part[NX // 2]
    along_x = ring_sum([part[0], part[1], None, part[3]], (half[: NB // 2], half[NB // 2 :]), AX, NX)
    pair = next(along_x)
    both, pair = tied(gather(both.reshape(NB, PW + ROWS_DEV), AX, NX), pair)
    both = both.reshape(PW, PW + ROWS_DEV)
    pair = along_x.send(pair)
    matrix = matrix_slab + along_x.send(pair)
    with jax.named_scope("slab_swap"):
        offer = jnp.concatenate([dot_nt(matrix, pick), matrix[:, :PW]], axis=1)
        diag = lax.optimization_barrier((both[:, :PW], offer))[0]
        offers = gather(offer, AY, PROW)
    packed, loinv, upinv = factor(diag)
    return finish(pivot[:, None], matrix, offers, both[:, PW:], packed, loinv, upinv)


def solution(mesh):
    torus = Mesh(mesh.devices.reshape(mesh.shape["prow"], NX, NZ), (AY, AX, AZ))
    placed = (
        P(PCOL, AY),
        P(AY, PCOL, None, None),
        P(AY, PCOL),
        P(AY, PCOL),
        P(AY, PCOL),
        P(),
    )
    return jax.shard_map(
        per_device, mesh=torus, in_specs=placed, out_specs=P(PCOL, AY), check_vma=False
    )
```

```python
import functools

import jax
import jax.numpy as jnp
from jax import lax
from jax.experimental import pallas as pl
from jax.experimental.pallas import tpu as pltpu
from jax.sharding import Mesh
from jax.sharding import PartitionSpec as P

SLAB = 2048
PW = 256
NB = 64
TR = 256
CB_DEV = 32
NX = 4
NZ = 8
PROW = 8
OWNERS = PW // NB
ROWS_DEV = 512
G = 8
AX, AZ, AY = "pcol_0", "pcol_1", "prow"
PCOL = (AX, AZ)
HIGHEST = lax.Precision.HIGHEST
F32 = jnp.float32
MIB = 1024 * 1024
VMEM = pl.BlockSpec(memory_space=pltpu.VMEM)
SMEM = pl.BlockSpec(memory_space=pltpu.SMEM)
HBM = pl.BlockSpec(memory_space=pltpu.HBM)


def dotf(a, b):
    return jnp.dot(a, b, precision=HIGHEST, preferred_element_type=F32)


def dot_nt(a, b):
    dims = (((1,), (1,)), ((), ()))
    return lax.dot_general(a, b, dims, precision=HIGHEST, preferred_element_type=F32)


CH = 8


def scatter_kernel(tc_ref, tr_ref, lr_ref, blocks_ref, slab_ref, pan_out, *rest):
    dense_outs = rest[:NZ]
    tc, tr, lr, own, buf, dense, pan, in_sem, num_sem, out_sem = rest[NZ:]
    my_x = lax.axis_index(AX)
    my_z = lax.axis_index(AZ)
    owner = (my_x == 0) & (my_z < OWNERS)
    numbers = [
        pltpu.make_async_copy(src, dst, num_sem.at[i])
        for i, (src, dst) in enumerate(((tc_ref, tc), (tr_ref, tr), (lr_ref, lr), (slab_ref, own)))
    ]
    for number in numbers:
        number.start()
    loads = [
        pltpu.make_async_copy(blocks_ref.at[pl.ds(i * CH, CH)], buf.at[pl.ds(i * CH, CH)], in_sem.at[i])
        for i in range(CB_DEV // CH)
    ]
    for load in loads:
        load.start()

    def clear(i, carry):
        dense[i] = jnp.zeros((NB, ROWS_DEV), F32)
        return carry

    lax.fori_loop(0, NX * NZ, clear, 0)
    for number in numbers:
        number.wait()
    for i in range(OWNERS):
        pan[i] = jnp.where(owner & (my_z == i), own[...], 0.0)
    lane = lax.broadcasted_iota(jnp.int32, (NB, TR), 1)

    def add(i, carry):
        col = tc[0, i]
        at = pl.ds(pl.multiple_of(tr[0, i] * TR, TR), TR)
        block = jnp.where(lane < lr[0, i], buf[i], 0.0)

        @pl.when(col < OWNERS)
        def _():
            pan[col, :, at] = pan[col, :, at] + block

        @pl.when(col >= OWNERS)
        def _():
            slot = ((col % NZ + NZ - my_z) % NZ) * NX + (col // NZ + NX - my_x) % NX
            dense[slot, :, at] = dense[slot, :, at] + block

        return carry

    for i in range(CB_DEV // CH):
        loads[i].wait()
        lax.fori_loop(i * CH, (i + 1) * CH, add, 0)
    stores = [pltpu.make_async_copy(pan, pan_out, out_sem.at[0])]
    base = 0
    for i, out in enumerate(dense_outs):
        stores.append(pltpu.make_async_copy(dense.at[pl.ds(base, out.shape[0])], out, out_sem.at[1 + i]))
        base += out.shape[0]
    for store in stores:
        store.start()
    for store in stores:
        store.wait()


def scatter(tc, tr, lr, blocks, slab):
    sizes = [NX] * NZ
    outs = pl.pallas_call(
        scatter_kernel,
        out_shape=[jax.ShapeDtypeStruct((n, NB, ROWS_DEV), F32) for n in [OWNERS] + sizes],
        in_specs=[HBM] * 5,
        out_specs=[HBM] * (1 + NZ),
        scratch_shapes=[pltpu.SMEM((1, CB_DEV), jnp.int32)] * 3
        + [
            pltpu.VMEM((NB, ROWS_DEV), F32),
            pltpu.VMEM((CB_DEV, NB, TR), F32),
            pltpu.VMEM((NX * NZ, NB, ROWS_DEV), F32),
            pltpu.VMEM((OWNERS, NB, ROWS_DEV), F32),
            pltpu.SemaphoreType.DMA((CB_DEV // CH,)),
            pltpu.SemaphoreType.DMA((4,)),
            pltpu.SemaphoreType.DMA((1 + NZ,)),
        ],
        compiler_params=pltpu.CompilerParams(vmem_limit_bytes=56 * MIB),
        name="scatter",
    )(tc, tr, lr, blocks, slab)
    return outs[0], list(outs[1:])


def shift(value, axis, n, step):
    return lax.ppermute(value, axis, [(i, (i + step) % n) for i in range(n)])


def ring_sum(rel, axis, n):
    ahead, back = yield [shift(rel[n // 2], axis, n, 1), shift(rel[n // 2 + 1], axis, n, -1)]
    for d in range(n // 2 - 1, 0, -1):
        sent = [shift(rel[d] + ahead, axis, n, 1)]
        if d > 1:
            sent.append(shift(rel[n - d + 1] + back, axis, n, -1))
            ahead, back = yield sent
        else:
            (ahead,) = yield sent
    yield rel[0] + back + ahead


def tied(value, sent):
    return value, lax.optimization_barrier((value, *sent))[1:]


def exchange(value, axis):
    return lax.all_to_all(value, axis, split_axis=0, concat_axis=0, tiled=True)


def copied(value, n):
    return jnp.broadcast_to(value, (n, *value.shape))


def gather(value, axis, n):
    return exchange(copied(value, n), axis)


def factor_kernel(t_ref, packed_ref, loinv_ref, upinv_ref, x_ref, v_ref, r_ref, lo_ref, ti_ref, b_ref):
    x_ref[...] = t_ref[...]
    b_ref[...] = jnp.zeros_like(b_ref)
    ti_ref[...] = jnp.zeros_like(ti_ref)
    lo_ref[...] = jnp.zeros_like(lo_ref)
    r_ref[...] = jnp.zeros_like(r_ref)
    lane = lax.broadcasted_iota(jnp.int32, (G, PW), 1)
    row8 = lax.broadcasted_iota(jnp.int32, (G, 128), 0)
    row = lax.broadcasted_iota(jnp.int32, (G, PW), 0)
    lane1 = lax.broadcasted_iota(jnp.int32, (1, PW), 1)
    panel = t_ref[0:G, :]
    steps = PW // G
    for b in range(steps):
        k0 = G * b
        inblk = (lane >= k0) & (lane < k0 + G)
        cols = [jnp.broadcast_to(panel[:, k0 + j : k0 + j + 1], (G, 128)) for j in range(G)]
        nxt = None
        if b + 1 < steps:
            below = x_ref[k0 + G : k0 + 2 * G, :]
            mult = [jnp.broadcast_to(below[:, k0 + j : k0 + j + 1], (G, PW)) for j in range(G)]
            nxt = jnp.where(inblk, 0.0, below)
        lo_block = jnp.zeros((G, PW), F32)
        for k in range(G):
            ck = cols[k]
            inv = 1.0 / jnp.broadcast_to(ck[k : k + 1, :], (G, 128))
            inv2 = jnp.concatenate([inv, inv], axis=1)
            ck2 = jnp.concatenate([ck, ck], axis=1)
            for j in range(k + 1, G):
                m = jnp.broadcast_to(cols[j][k : k + 1, :], (G, 128)) * inv
                cols[j] = jnp.where(row8 == k, m, cols[j] - ck * m)
            lo_block = jnp.where((lane == k0 + k) & (row >= k), ck2, lo_block)
            panel = jnp.where(lane == k0 + k, jnp.where(row == k, 1.0, 0.0), panel)
            scaled = jnp.broadcast_to(panel[k : k + 1, :], (G, PW)) * inv2
            v_ref[k0 + k : k0 + k + 1, :] = scaled[0:1]
            panel = jnp.where(row == k, scaled, panel - ck2 * scaled)
        lo_ref[k0 : k0 + G, :] = lo_block
        ti_ref[k0 : k0 + G, :] = jnp.where(inblk, panel, 0.0)
        if nxt is not None:
            for j in range(G):
                nxt = nxt - mult[j] * jnp.broadcast_to(panel[j : j + 1, :], (G, PW))
        tile = (k0 // 128) * 128
        kk = k0 % 128
        slot = b % 2
        if b >= 2:
            old = (k0 - 2 * G) % 128
            b_ref[slot, old : old + G, :] = jnp.zeros((G, PW), F32)
        b_ref[slot, kk : kk + G, :] = panel
        inb = (lane1 >= k0) & (lane1 < k0 + G)
        raw = x_ref[:, tile : tile + 128]
        r_ref[:, tile : tile + 128] = jnp.where(inb[:, tile : tile + 128], raw, r_ref[:, tile : tile + 128])
        if b + 1 < steps:
            x_ref[...] = jnp.where(inb, 0.0, x_ref[...]) - dotf(raw, b_ref[slot])
            x_ref[k0 : k0 + G, :] = -panel
        unit = jnp.where(row == lane - k0, 1.0, 0.0)
        r_ref[k0 : k0 + G, :] = jnp.where(inblk, unit, r_ref[k0 : k0 + G, :])
        panel = nxt
    z = dotf(r_ref[...], dotf(ti_ref[...], lo_ref[...]))
    v = v_ref[...]
    rr = lax.broadcasted_iota(jnp.int32, (PW, PW), 0)
    cc = lax.broadcasted_iota(jnp.int32, (PW, PW), 1)
    same = (rr // G) == (cc // G)
    packed_ref[...] = jnp.where(rr < cc, v, jnp.where(same, lo_ref[...], z))
    loinv_ref[...] = jnp.where(rr >= cc, v, 0.0)
    upinv_ref[...] = jnp.where(rr < cc, z, jnp.where(rr == cc, 1.0, 0.0))


def factor(t):
    return pl.pallas_call(
        factor_kernel,
        out_shape=[jax.ShapeDtypeStruct((PW, PW), F32)] * 3,
        in_specs=[VMEM],
        out_specs=[VMEM] * 3,
        scratch_shapes=[pltpu.VMEM((PW, PW), F32)] * 5 + [pltpu.VMEM((2, 128, PW), F32)],
        compiler_params=pltpu.CompilerParams(vmem_limit_bytes=16 * MIB),
        cost_estimate=pl.CostEstimate(flops=40_000_000, bytes_accessed=60_000_000, transcendentals=0),
        name="factor",
    )(t)


def finish_kernel(pivot_ref, matrix_ref, offers_ref, panel_ref, packed_ref, loinv_ref, upinv_ref, out_ref, low_ref):
    row_group = lax.axis_index(AY)
    col_group = lax.axis_index(AX) * NZ + lax.axis_index(AZ)
    rows = lax.broadcasted_iota(jnp.int32, (PW, ROWS_DEV), 1) + row_group * ROWS_DEV
    pick = jnp.where(pivot_ref[...] == rows, 1.0, 0.0)
    hit = jnp.sum(pick, axis=0, keepdims=True) > 0.0
    low_ref[...] = dotf(loinv_ref[...], panel_ref[...])
    matrix = jnp.where(hit, dotf(offers_ref[0, :, PW:], pick), matrix_ref[...])
    inc = offers_ref[0, :, :PW]
    for i in range(1, PROW):
        inc = inc + offers_ref[i, :, :PW]
    upper = dotf(inc, upinv_ref[...])
    out_ref[...] = matrix - dotf(upper, low_ref[...])

    @pl.when(row_group == 0)
    def _():
        out_ref[:, :PW] = upper

    @pl.when(col_group < OWNERS)
    def _():
        at = pl.ds(pl.multiple_of(col_group * NB, NB), NB)
        out_ref[...] = low_ref[at, :]

        @pl.when(row_group == 0)
        def _():
            out_ref[:, :PW] = packed_ref[at, :]


def finish(pivot, matrix, offers, panel, packed, loinv, upinv):
    return pl.pallas_call(
        finish_kernel,
        out_shape=jax.ShapeDtypeStruct((NB, ROWS_DEV), F32),
        in_specs=[VMEM] * 7,
        out_specs=VMEM,
        scratch_shapes=[pltpu.VMEM((PW, ROWS_DEV), F32)],
        compiler_params=pltpu.CompilerParams(vmem_limit_bytes=16 * MIB),
        name="finish",
    )(pivot, matrix, offers, panel, packed, loinv, upinv)


def per_device(matrix_slab, contributions, target_column, target_rows, live_rows, pivot_index):
    row_group = lax.axis_index(AY)
    pan, dense = scatter(target_column, target_rows, live_rows, contributions[0], matrix_slab)
    pivot = pivot_index[0]
    pick = (pivot[:, None] == row_group * ROWS_DEV + jnp.arange(ROWS_DEV)[None, :]).astype(F32)
    hit = jnp.sum(pick, axis=0) > 0

    along_z = ring_sum(dense, AZ, NZ)
    pair = next(along_z)
    chunk = exchange(pan, AX).sum(axis=0).reshape(NZ, NB // NZ, ROWS_DEV)
    chunk, pair = tied(chunk, pair)
    pair = along_z.send(pair)
    chunk = exchange(chunk, AZ).sum(axis=0)
    offer = jnp.concatenate([dot_nt(chunk, pick), chunk[:, :PW]], axis=1)
    offers, pair = tied(copied(offer, PROW), pair)
    pair = along_z.send(pair)
    offers = exchange(offers, AY)
    moved = offers[0, :, PW:]
    chunk = jnp.where(hit[None, :], dotf(moved, pick), chunk)
    both = jnp.concatenate([offers[:, :, :PW].sum(axis=0), chunk], axis=1)
    both = exchange(copied(both, NZ), AZ).reshape(NB, PW + ROWS_DEV)
    both, pair = tied(both, pair)
    pair = along_z.send(pair)
    both, pair = tied(copied(both, NX), pair)
    along_x = ring_sum(along_z.send(pair), AX, NX)
    pair = next(along_x)
    both, pair = tied(exchange(both, AX).reshape(PW, PW + ROWS_DEV), pair)
    pair = along_x.send(pair)
    matrix = matrix_slab + along_x.send(pair)
    with jax.named_scope("slab_swap"):
        offer = jnp.concatenate([dot_nt(matrix, pick), matrix[:, :PW]], axis=1)
        diag = lax.optimization_barrier((both[:, :PW], offer))[0]
        offers = gather(offer, AY, PROW)
    packed, loinv, upinv = factor(diag)
    return finish(pivot[:, None], matrix, offers, both[:, PW:], packed, loinv, upinv)


def solution(mesh):
    torus = Mesh(mesh.devices.reshape(mesh.shape["prow"], NX, NZ), (AY, AX, AZ))
    placed = (
        P(PCOL, AY),
        P(AY, PCOL, None, None),
        P(AY, PCOL),
        P(AY, PCOL),
        P(AY, PCOL),
        P(),
    )
    return jax.shard_map(
        per_device, mesh=torus, in_specs=placed, out_specs=P(PCOL, AY), check_vma=False
    )
```

```python
import functools

import jax
import jax.numpy as jnp
from jax import lax
from jax.experimental import pallas as pl
from jax.experimental.pallas import tpu as pltpu
from jax.sharding import Mesh
from jax.sharding import PartitionSpec as P

SLAB = 2048
PW = 256
NB = 64
TR = 256
CB_DEV = 32
NX = 4
NZ = 8
PROW = 8
OWNERS = PW // NB
ROWS_DEV = 512
G = 8
AX, AZ, AY = "pcol_0", "pcol_1", "prow"
PCOL = (AX, AZ)
HIGHEST = lax.Precision.HIGHEST
F32 = jnp.float32
MIB = 1024 * 1024
VMEM = pl.BlockSpec(memory_space=pltpu.VMEM)
SMEM = pl.BlockSpec(memory_space=pltpu.SMEM)
HBM = pl.BlockSpec(memory_space=pltpu.HBM)


def dotf(a, b):
    return jnp.dot(a, b, precision=HIGHEST, preferred_element_type=F32)


def dot_nt(a, b):
    dims = (((1,), (1,)), ((), ()))
    return lax.dot_general(a, b, dims, precision=HIGHEST, preferred_element_type=F32)


CH = 8


def start_loads(sources, targets, sems):
    copies = [pltpu.make_async_copy(src, dst, sems.at[i]) for i, (src, dst) in enumerate(zip(sources, targets))]
    for copy in copies:
        copy.start()
    return copies


def add_blocks(numbers, loads, buf, place):
    tc, tr, lr = numbers
    lane = lax.broadcasted_iota(jnp.int32, (NB, TR), 1)

    def add(i, carry):
        at = pl.ds(pl.multiple_of(tr[0, i] * TR, TR), TR)
        place(tc[0, i], at, lambda: jnp.where(lane < lr[0, i], buf[i], 0.0))
        return carry

    for i in range(CB_DEV // CH):
        loads[i].wait()
        lax.fori_loop(i * CH, (i + 1) * CH, add, 0)


def parts_of(ref):
    return [ref.at[pl.ds(i * CH, CH)] for i in range(CB_DEV // CH)]


def panel_kernel(tc_ref, tr_ref, lr_ref, blocks_ref, slab_ref, pan_out, tc, tr, lr, own, buf, pan, in_sem, num_sem, out_sem):
    my_z = lax.axis_index(AZ)
    owner = (lax.axis_index(AX) == 0) & (my_z < OWNERS)
    numbers = start_loads((tc_ref, tr_ref, lr_ref, slab_ref), (tc, tr, lr, own), num_sem)
    loads = start_loads(parts_of(blocks_ref), parts_of(buf), in_sem)
    for number in numbers:
        number.wait()
    for i in range(OWNERS):
        pan[i] = jnp.where(owner & (my_z == i), own[...], 0.0)

    def place(col, at, block):
        @pl.when(col < OWNERS)
        def _():
            pan[col, :, at] = pan[col, :, at] + block()

    add_blocks((tc, tr, lr), loads, buf, place)
    store = pltpu.make_async_copy(pan, pan_out, out_sem.at[0])
    store.start()
    store.wait()


def dense_kernel(tc_ref, tr_ref, lr_ref, blocks_ref, *rest):
    dense_outs = rest[: NZ + 1]
    tc, tr, lr, buf, dense, in_sem, num_sem, out_sem = rest[NZ + 1 :]
    my_x = lax.axis_index(AX)
    my_z = lax.axis_index(AZ)
    numbers = start_loads((tc_ref, tr_ref, lr_ref), (tc, tr, lr), num_sem)
    loads = start_loads(parts_of(blocks_ref), parts_of(buf), in_sem)

    def clear(i, carry):
        dense[i] = jnp.zeros((NB, ROWS_DEV), F32)
        return carry

    lax.fori_loop(0, NX * NZ, clear, 0)
    for number in numbers:
        number.wait()

    def place(col, at, block):
        @pl.when(col >= OWNERS)
        def _():
            slot = ((col % NZ + NZ - my_z) % NZ) * NX + (col // NZ + NX - my_x) % NX
            dense[slot, :, at] = dense[slot, :, at] + block()

    add_blocks((tc, tr, lr), loads, buf, place)
    pieces, base = [], 0
    for out in dense_outs:
        pieces.append(dense.at[pl.ds(base, out.shape[0])])
        base += out.shape[0]
    stores = start_loads(pieces, dense_outs, out_sem)
    for store in stores:
        store.wait()


def scatter(tc, tr, lr, blocks, slab):
    loads = pltpu.SemaphoreType.DMA((CB_DEV // CH,))
    numbers = [pltpu.SMEM((1, CB_DEV), jnp.int32)] * 3
    buf = pltpu.VMEM((CB_DEV, NB, TR), F32)
    params = pltpu.CompilerParams(vmem_limit_bytes=56 * MIB)
    pan = pl.pallas_call(
        panel_kernel,
        out_shape=jax.ShapeDtypeStruct((OWNERS, NB, ROWS_DEV), F32),
        in_specs=[HBM] * 5,
        out_specs=HBM,
        scratch_shapes=numbers
        + [pltpu.VMEM((NB, ROWS_DEV), F32), buf, pltpu.VMEM((OWNERS, NB, ROWS_DEV), F32), loads]
        + [pltpu.SemaphoreType.DMA((4,)), pltpu.SemaphoreType.DMA((1,))],
        compiler_params=params,
        cost_estimate=pl.CostEstimate(flops=1_000_000, bytes_accessed=3_000_000, transcendentals=0),
        name="panel_blocks",
    )(tc, tr, lr, blocks, slab)
    dense = pl.pallas_call(
        dense_kernel,
        out_shape=[jax.ShapeDtypeStruct((n, NB, ROWS_DEV), F32) for n in [NX] * 4 + [NX // 2] * 2 + [NX] * 3],
        in_specs=[HBM] * 4,
        out_specs=[HBM] * (NZ + 1),
        scratch_shapes=numbers
        + [buf, pltpu.VMEM((NX * NZ, NB, ROWS_DEV), F32), loads]
        + [pltpu.SemaphoreType.DMA((3,)), pltpu.SemaphoreType.DMA((NZ + 1,))],
        compiler_params=params,
        cost_estimate=pl.CostEstimate(flops=1_000_000, bytes_accessed=40_000_000, transcendentals=0),
        name="slab_blocks",
    )(tc, tr, lr, blocks)
    return pan, list(dense)


def shift(value, axis, n, step):
    return lax.ppermute(value, axis, [(i, (i + step) % n) for i in range(n)])


def ring_sum(rel, axis, n):
    ahead, back = yield [shift(rel[n // 2], axis, n, 1), shift(rel[n // 2 + 1], axis, n, -1)]
    for d in range(n // 2 - 1, 0, -1):
        sent = [shift(rel[d] + ahead, axis, n, 1)]
        if d > 1:
            sent.append(shift(rel[n - d + 1] + back, axis, n, -1))
            ahead, back = yield sent
        else:
            (ahead,) = yield sent
    yield rel[0] + back + ahead


def ring_sum_halves(rel, halves, axis, n):
    h = halves[0].shape[0]
    ahead, back = yield [shift(halves[0], axis, n, 1), shift(halves[1], axis, n, -1)]
    for d in range(n // 2 - 1, 0, -1):
        up, down = rel[d], rel[n - d]
        if d == n // 2 - 1:
            up = jnp.concatenate([up[:h] + ahead, up[h:]], axis=0)
            down = jnp.concatenate([down[:h], down[h:] + back], axis=0)
        else:
            up, down = up + ahead, down + back
        ahead, back = yield [shift(up, axis, n, 1), shift(down, axis, n, -1)]
    yield rel[0] + ahead + back


def tied(value, sent):
    return value, lax.optimization_barrier((value, *sent))[1:]


def exchange(value, axis):
    return lax.all_to_all(value, axis, split_axis=0, concat_axis=0, tiled=True)


def copied(value, n):
    return jnp.broadcast_to(value, (n, *value.shape))


def gather(value, axis, n):
    return exchange(copied(value, n), axis)


def factor_kernel(t_ref, packed_ref, loinv_ref, upinv_ref, x_ref, v_ref, r_ref, lo_ref, ti_ref, b_ref):
    x_ref[...] = t_ref[...]
    b_ref[...] = jnp.zeros_like(b_ref)
    ti_ref[...] = jnp.zeros_like(ti_ref)
    lo_ref[...] = jnp.zeros_like(lo_ref)
    r_ref[...] = jnp.zeros_like(r_ref)
    lane = lax.broadcasted_iota(jnp.int32, (G, PW), 1)
    row8 = lax.broadcasted_iota(jnp.int32, (G, 128), 0)
    row = lax.broadcasted_iota(jnp.int32, (G, PW), 0)
    lane1 = lax.broadcasted_iota(jnp.int32, (1, PW), 1)
    panel = t_ref[0:G, :]
    steps = PW // G
    for b in range(steps):
        k0 = G * b
        inblk = (lane >= k0) & (lane < k0 + G)
        cols = [jnp.broadcast_to(panel[:, k0 + j : k0 + j + 1], (G, 128)) for j in range(G)]
        nxt = None
        if b + 1 < steps:
            below = x_ref[k0 + G : k0 + 2 * G, :]
            mult = [jnp.broadcast_to(below[:, k0 + j : k0 + j + 1], (G, PW)) for j in range(G)]
            nxt = jnp.where(inblk, 0.0, below)
        lo_block = jnp.zeros((G, PW), F32)
        for k in range(G):
            ck = cols[k]
            inv = 1.0 / jnp.broadcast_to(ck[k : k + 1, :], (G, 128))
            inv2 = jnp.concatenate([inv, inv], axis=1)
            ck2 = jnp.concatenate([ck, ck], axis=1)
            for j in range(k + 1, G):
                m = jnp.broadcast_to(cols[j][k : k + 1, :], (G, 128)) * inv
                cols[j] = jnp.where(row8 == k, m, cols[j] - ck * m)
            lo_block = jnp.where((lane == k0 + k) & (row >= k), ck2, lo_block)
            panel = jnp.where(lane == k0 + k, jnp.where(row == k, 1.0, 0.0), panel)
            scaled = jnp.broadcast_to(panel[k : k + 1, :], (G, PW)) * inv2
            v_ref[k0 + k : k0 + k + 1, :] = scaled[0:1]
            panel = jnp.where(row == k, scaled, panel - ck2 * scaled)
        lo_ref[k0 : k0 + G, :] = lo_block
        ti_ref[k0 : k0 + G, :] = jnp.where(inblk, panel, 0.0)
        if nxt is not None:
            for j in range(G):
                nxt = nxt - mult[j] * jnp.broadcast_to(panel[j : j + 1, :], (G, PW))
        tile = (k0 // 128) * 128
        kk = k0 % 128
        slot = b % 2
        if b >= 2:
            old = (k0 - 2 * G) % 128
            b_ref[slot, old : old + G, :] = jnp.zeros((G, PW), F32)
        b_ref[slot, kk : kk + G, :] = panel
        inb = (lane1 >= k0) & (lane1 < k0 + G)
        raw = x_ref[:, tile : tile + 128]
        r_ref[:, tile : tile + 128] = jnp.where(inb[:, tile : tile + 128], raw, r_ref[:, tile : tile + 128])
        if b + 1 < steps:
            x_ref[...] = jnp.where(inb, 0.0, x_ref[...]) - dotf(raw, b_ref[slot])
            x_ref[k0 : k0 + G, :] = -panel
        unit = jnp.where(row == lane - k0, 1.0, 0.0)
        r_ref[k0 : k0 + G, :] = jnp.where(inblk, unit, r_ref[k0 : k0 + G, :])
        panel = nxt
    z = dotf(r_ref[...], dotf(ti_ref[...], lo_ref[...]))
    v = v_ref[...]
    rr = lax.broadcasted_iota(jnp.int32, (PW, PW), 0)
    cc = lax.broadcasted_iota(jnp.int32, (PW, PW), 1)
    same = (rr // G) == (cc // G)
    packed_ref[...] = jnp.where(rr < cc, v, jnp.where(same, lo_ref[...], z))
    loinv_ref[...] = jnp.where(rr >= cc, v, 0.0)
    upinv_ref[...] = jnp.where(rr < cc, z, jnp.where(rr == cc, 1.0, 0.0))


def factor(t):
    return pl.pallas_call(
        factor_kernel,
        out_shape=[jax.ShapeDtypeStruct((PW, PW), F32)] * 3,
        in_specs=[VMEM],
        out_specs=[VMEM] * 3,
        scratch_shapes=[pltpu.VMEM((PW, PW), F32)] * 5 + [pltpu.VMEM((2, 128, PW), F32)],
        compiler_params=pltpu.CompilerParams(vmem_limit_bytes=16 * MIB),
        cost_estimate=pl.CostEstimate(flops=40_000_000, bytes_accessed=60_000_000, transcendentals=0),
        name="factor",
    )(t)


def finish_kernel(pivot_ref, matrix_ref, offers_ref, panel_ref, packed_ref, loinv_ref, upinv_ref, out_ref, low_ref):
    row_group = lax.axis_index(AY)
    col_group = lax.axis_index(AX) * NZ + lax.axis_index(AZ)
    rows = lax.broadcasted_iota(jnp.int32, (PW, ROWS_DEV), 1) + row_group * ROWS_DEV
    pick = jnp.where(pivot_ref[...] == rows, 1.0, 0.0)
    hit = jnp.sum(pick, axis=0, keepdims=True) > 0.0
    low_ref[...] = dotf(loinv_ref[...], panel_ref[...])
    matrix = jnp.where(hit, dotf(offers_ref[0, :, PW:], pick), matrix_ref[...])
    inc = offers_ref[0, :, :PW]
    for i in range(1, PROW):
        inc = inc + offers_ref[i, :, :PW]
    upper = dotf(inc, upinv_ref[...])
    out_ref[...] = matrix - dotf(upper, low_ref[...])

    @pl.when(row_group == 0)
    def _():
        out_ref[:, :PW] = upper

    @pl.when(col_group < OWNERS)
    def _():
        at = pl.ds(pl.multiple_of(col_group * NB, NB), NB)
        out_ref[...] = low_ref[at, :]

        @pl.when(row_group == 0)
        def _():
            out_ref[:, :PW] = packed_ref[at, :]


def finish(pivot, matrix, offers, panel, packed, loinv, upinv):
    return pl.pallas_call(
        finish_kernel,
        out_shape=jax.ShapeDtypeStruct((NB, ROWS_DEV), F32),
        in_specs=[VMEM] * 7,
        out_specs=VMEM,
        scratch_shapes=[pltpu.VMEM((PW, ROWS_DEV), F32)],
        compiler_params=pltpu.CompilerParams(vmem_limit_bytes=16 * MIB),
        name="finish",
    )(pivot, matrix, offers, panel, packed, loinv, upinv)


def per_device(matrix_slab, contributions, target_column, target_rows, live_rows, pivot_index):
    row_group = lax.axis_index(AY)
    pan, dense = scatter(target_column, target_rows, live_rows, contributions[0], matrix_slab)
    pivot = pivot_index[0]
    pick = (pivot[:, None] == row_group * ROWS_DEV + jnp.arange(ROWS_DEV)[None, :]).astype(F32)
    hit = jnp.sum(pick, axis=0) > 0

    along_z = ring_sum_halves(dense[:4] + [None] + dense[6:], dense[4:6], AZ, NZ)
    pair = next(along_z)
    chunk = exchange(pan, AX).sum(axis=0).reshape(NZ, NB // NZ, ROWS_DEV)
    chunk, pair = tied(chunk, pair)
    pair = along_z.send(pair)
    chunk = exchange(chunk, AZ).sum(axis=0)
    offer = jnp.concatenate([dot_nt(chunk, pick), chunk[:, :PW]], axis=1)
    offers, pair = tied(copied(offer, PROW), pair)
    pair = along_z.send(pair)
    offers = exchange(offers, AY)
    moved = offers[0, :, PW:]
    chunk = jnp.where(hit[None, :], dotf(moved, pick), chunk)
    both = jnp.concatenate([offers[:, :, :PW].sum(axis=0), chunk], axis=1)
    both = exchange(copied(both, NZ), AZ).reshape(NB, PW + ROWS_DEV)
    both, pair = tied(both, pair)
    pair = along_z.send(pair)
    both, pair = tied(copied(both, NX), pair)
    along_x = ring_sum(along_z.send(pair), AX, NX)
    pair = next(along_x)
    both, pair = tied(exchange(both, AX).reshape(PW, PW + ROWS_DEV), pair)
    pair = along_x.send(pair)
    matrix = matrix_slab + along_x.send(pair)
    with jax.named_scope("slab_swap"):
        offer = jnp.concatenate([dot_nt(matrix, pick), matrix[:, :PW]], axis=1)
        diag = lax.optimization_barrier((both[:, :PW], offer))[0]
        offers = gather(offer, AY, PROW)
    packed, loinv, upinv = factor(diag)
    return finish(pivot[:, None], matrix, offers, both[:, PW:], packed, loinv, upinv)


def solution(mesh):
    torus = Mesh(mesh.devices.reshape(mesh.shape["prow"], NX, NZ), (AY, AX, AZ))
    placed = (
        P(PCOL, AY),
        P(AY, PCOL, None, None),
        P(AY, PCOL),
        P(AY, PCOL),
        P(AY, PCOL),
        P(),
    )
    return jax.shard_map(
        per_device, mesh=torus, in_specs=placed, out_specs=P(PCOL, AY), check_vma=False
    )
```

```python
import functools

import jax
import jax.numpy as jnp
from jax import lax
from jax.experimental import pallas as pl
from jax.experimental.pallas import tpu as pltpu
from jax.sharding import Mesh
from jax.sharding import PartitionSpec as P

SLAB = 2048
PW = 256
NB = 64
TR = 256
CB_DEV = 32
NX = 4
NZ = 8
PROW = 8
OWNERS = PW // NB
ROWS_DEV = 512
G = 8
AX, AZ, AY = "pcol_0", "pcol_1", "prow"
PCOL = (AX, AZ)
HIGHEST = lax.Precision.HIGHEST
F32 = jnp.float32
MIB = 1024 * 1024
VMEM = pl.BlockSpec(memory_space=pltpu.VMEM)
SMEM = pl.BlockSpec(memory_space=pltpu.SMEM)
HBM = pl.BlockSpec(memory_space=pltpu.HBM)


def dotf(a, b):
    return jnp.dot(a, b, precision=HIGHEST, preferred_element_type=F32)


def dot_nt(a, b):
    dims = (((1,), (1,)), ((), ()))
    return lax.dot_general(a, b, dims, precision=HIGHEST, preferred_element_type=F32)


CH = 8


def start_loads(sources, targets, sems):
    copies = [pltpu.make_async_copy(src, dst, sems.at[i]) for i, (src, dst) in enumerate(zip(sources, targets))]
    for copy in copies:
        copy.start()
    return copies


def add_blocks(numbers, loads, buf, place):
    tc, tr, lr = numbers
    lane = lax.broadcasted_iota(jnp.int32, (NB, TR), 1)

    def add(i, carry):
        at = pl.ds(pl.multiple_of(tr[0, i] * TR, TR), TR)
        place(tc[0, i], at, lambda: jnp.where(lane < lr[0, i], buf[i], 0.0))
        return carry

    for i in range(CB_DEV // CH):
        loads[i].wait()
        lax.fori_loop(i * CH, (i + 1) * CH, add, 0)


def parts_of(ref):
    return [ref.at[pl.ds(i * CH, CH)] for i in range(CB_DEV // CH)]


def panel_kernel(tc_ref, tr_ref, lr_ref, blocks_ref, slab_ref, pan_out, tc, tr, lr, own, buf, pan, in_sem, num_sem, out_sem):
    my_z = lax.axis_index(AZ)
    owner = (lax.axis_index(AX) == 0) & (my_z < OWNERS)
    numbers = start_loads((tc_ref, tr_ref, lr_ref, slab_ref), (tc, tr, lr, own), num_sem)
    loads = start_loads(parts_of(blocks_ref), parts_of(buf), in_sem)
    for number in numbers:
        number.wait()
    for i in range(OWNERS):
        pan[i] = jnp.where(owner & (my_z == i), own[...], 0.0)

    def place(col, at, block):
        @pl.when(col < OWNERS)
        def _():
            pan[col, :, at] = pan[col, :, at] + block()

    add_blocks((tc, tr, lr), loads, buf, place)
    store = pltpu.make_async_copy(pan, pan_out, out_sem.at[0])
    store.start()
    store.wait()


def dense_kernel(tc_ref, tr_ref, lr_ref, blocks_ref, *rest):
    dense_outs = rest[: NZ + 1]
    tc, tr, lr, buf, dense, in_sem, num_sem, out_sem = rest[NZ + 1 :]
    my_x = lax.axis_index(AX)
    my_z = lax.axis_index(AZ)
    numbers = start_loads((tc_ref, tr_ref, lr_ref), (tc, tr, lr), num_sem)
    loads = start_loads(parts_of(blocks_ref), parts_of(buf), in_sem)

    def clear(i, carry):
        dense[i] = jnp.zeros((NB, ROWS_DEV), F32)
        return carry

    lax.fori_loop(0, NX * NZ, clear, 0)
    for number in numbers:
        number.wait()

    def place(col, at, block):
        @pl.when(col >= OWNERS)
        def _():
            slot = ((col % NZ + NZ - my_z) % NZ) * NX + (col // NZ + NX - my_x) % NX
            dense[slot, :, at] = dense[slot, :, at] + block()

    add_blocks((tc, tr, lr), loads, buf, place)
    pieces, base = [], 0
    for out in dense_outs:
        pieces.append(dense.at[pl.ds(base, out.shape[0])])
        base += out.shape[0]
    stores = start_loads(pieces, dense_outs, out_sem)
    for store in stores:
        store.wait()


def scatter(tc, tr, lr, blocks, slab):
    loads = pltpu.SemaphoreType.DMA((CB_DEV // CH,))
    numbers = [pltpu.SMEM((1, CB_DEV), jnp.int32)] * 3
    buf = pltpu.VMEM((CB_DEV, NB, TR), F32)
    params = pltpu.CompilerParams(vmem_limit_bytes=56 * MIB)
    pan = pl.pallas_call(
        panel_kernel,
        out_shape=jax.ShapeDtypeStruct((OWNERS, NB, ROWS_DEV), F32),
        in_specs=[HBM] * 5,
        out_specs=HBM,
        scratch_shapes=numbers
        + [pltpu.VMEM((NB, ROWS_DEV), F32), buf, pltpu.VMEM((OWNERS, NB, ROWS_DEV), F32), loads]
        + [pltpu.SemaphoreType.DMA((4,)), pltpu.SemaphoreType.DMA((1,))],
        compiler_params=params,
        cost_estimate=pl.CostEstimate(flops=1_000_000, bytes_accessed=3_000_000, transcendentals=0),
        name="panel_blocks",
    )(tc, tr, lr, blocks, slab)
    dense = pl.pallas_call(
        dense_kernel,
        out_shape=[jax.ShapeDtypeStruct((n, NB, ROWS_DEV), F32) for n in [NX] * 4 + [NX // 2] * 2 + [NX] * 3],
        in_specs=[HBM] * 4,
        out_specs=[HBM] * (NZ + 1),
        scratch_shapes=numbers
        + [buf, pltpu.VMEM((NX * NZ, NB, ROWS_DEV), F32), loads]
        + [pltpu.SemaphoreType.DMA((3,)), pltpu.SemaphoreType.DMA((NZ + 1,))],
        compiler_params=params,
        cost_estimate=pl.CostEstimate(flops=1_000_000, bytes_accessed=40_000_000, transcendentals=0),
        name="slab_blocks",
    )(tc, tr, lr, blocks)
    return pan, list(dense)


def shift(value, axis, n, step):
    return lax.ppermute(value, axis, [(i, (i + step) % n) for i in range(n)])


def ring_sum(rel, axis, n):
    ahead, back = yield [shift(rel[n // 2], axis, n, 1), shift(rel[n // 2 + 1], axis, n, -1)]
    for d in range(n // 2 - 1, 0, -1):
        sent = [shift(rel[d] + ahead, axis, n, 1)]
        if d > 1:
            sent.append(shift(rel[n - d + 1] + back, axis, n, -1))
            ahead, back = yield sent
        else:
            (ahead,) = yield sent
    yield rel[0] + back + ahead


def ring_sum_halves(rel, halves, axis, n):
    h = halves[0].shape[0]
    ahead, back = yield [shift(halves[0], axis, n, 1), shift(halves[1], axis, n, -1)]
    for d in range(n // 2 - 1, 0, -1):
        up, down = rel[d], rel[n - d]
        if d == n // 2 - 1:
            up = jnp.concatenate([up[:h] + ahead, up[h:]], axis=0)
            down = jnp.concatenate([down[:h], down[h:] + back], axis=0)
        else:
            up, down = up + ahead, down + back
        ahead, back = yield [shift(up, axis, n, 1), shift(down, axis, n, -1)]
    yield rel[0] + ahead + back


def tied(value, sent):
    return value, lax.optimization_barrier((value, *sent))[1:]


def exchange(value, axis):
    return lax.all_to_all(value, axis, split_axis=0, concat_axis=0, tiled=True)


def copied(value, n):
    return jnp.broadcast_to(value, (n, *value.shape))


def gather(value, axis, n):
    return exchange(copied(value, n), axis)


def factor_kernel(t_ref, packed_ref, loinv_ref, upinv_ref, x_ref, v_ref, r_ref, lo_ref, ti_ref, b_ref):
    x_ref[...] = t_ref[...]
    b_ref[...] = jnp.zeros_like(b_ref)
    ti_ref[...] = jnp.zeros_like(ti_ref)
    lo_ref[...] = jnp.zeros_like(lo_ref)
    r_ref[...] = jnp.zeros_like(r_ref)
    lane = lax.broadcasted_iota(jnp.int32, (G, PW), 1)
    row8 = lax.broadcasted_iota(jnp.int32, (G, 128), 0)
    row = lax.broadcasted_iota(jnp.int32, (G, PW), 0)
    lane1 = lax.broadcasted_iota(jnp.int32, (1, PW), 1)
    panel = t_ref[0:G, :]
    steps = PW // G
    for b in range(steps):
        k0 = G * b
        inblk = (lane >= k0) & (lane < k0 + G)
        cols = [jnp.broadcast_to(panel[:, k0 + j : k0 + j + 1], (G, 128)) for j in range(G)]
        nxt = None
        if b + 1 < steps:
            below = x_ref[k0 + G : k0 + 2 * G, :]
            mult = [jnp.broadcast_to(below[:, k0 + j : k0 + j + 1], (G, PW)) for j in range(G)]
            nxt = jnp.where(inblk, 0.0, below)
        lo_block = jnp.zeros((G, PW), F32)
        for k in range(G):
            ck = cols[k]
            inv = 1.0 / jnp.broadcast_to(ck[k : k + 1, :], (G, 128))
            inv2 = jnp.concatenate([inv, inv], axis=1)
            ck2 = jnp.concatenate([ck, ck], axis=1)
            for j in range(k + 1, G):
                m = jnp.broadcast_to(cols[j][k : k + 1, :], (G, 128)) * inv
                cols[j] = jnp.where(row8 == k, m, cols[j] - ck * m)
            lo_block = jnp.where((lane == k0 + k) & (row >= k), ck2, lo_block)
            panel = jnp.where(lane == k0 + k, jnp.where(row == k, 1.0, 0.0), panel)
            scaled = jnp.broadcast_to(panel[k : k + 1, :], (G, PW)) * inv2
            v_ref[k0 + k : k0 + k + 1, :] = scaled[0:1]
            panel = jnp.where(row == k, scaled, panel - ck2 * scaled)
        lo_ref[k0 : k0 + G, :] = lo_block
        ti_ref[k0 : k0 + G, :] = jnp.where(inblk, panel, 0.0)
        if nxt is not None:
            for j in range(G):
                nxt = nxt - mult[j] * jnp.broadcast_to(panel[j : j + 1, :], (G, PW))
        tile = (k0 // 128) * 128
        kk = k0 % 128
        slot = b % 2
        if b >= 2:
            old = (k0 - 2 * G) % 128
            b_ref[slot, old : old + G, :] = jnp.zeros((G, PW), F32)
        b_ref[slot, kk : kk + G, :] = panel
        inb = (lane1 >= k0) & (lane1 < k0 + G)
        raw = x_ref[:, tile : tile + 128]
        r_ref[:, tile : tile + 128] = jnp.where(inb[:, tile : tile + 128], raw, r_ref[:, tile : tile + 128])
        if b + 1 < steps:
            x_ref[...] = jnp.where(inb, 0.0, x_ref[...]) - dotf(raw, b_ref[slot])
            x_ref[k0 : k0 + G, :] = -panel
        unit = jnp.where(row == lane - k0, 1.0, 0.0)
        r_ref[k0 : k0 + G, :] = jnp.where(inblk, unit, r_ref[k0 : k0 + G, :])
        panel = nxt
    z = dotf(r_ref[...], dotf(ti_ref[...], lo_ref[...]))
    v = v_ref[...]
    rr = lax.broadcasted_iota(jnp.int32, (PW, PW), 0)
    cc = lax.broadcasted_iota(jnp.int32, (PW, PW), 1)
    same = (rr // G) == (cc // G)
    packed_ref[...] = jnp.where(rr < cc, v, jnp.where(same, lo_ref[...], z))
    loinv_ref[...] = jnp.where(rr >= cc, v, 0.0)
    upinv_ref[...] = jnp.where(rr < cc, z, jnp.where(rr == cc, 1.0, 0.0))


def factor(t):
    return pl.pallas_call(
        factor_kernel,
        out_shape=[jax.ShapeDtypeStruct((PW, PW), F32)] * 3,
        in_specs=[VMEM],
        out_specs=[VMEM] * 3,
        scratch_shapes=[pltpu.VMEM((PW, PW), F32)] * 5 + [pltpu.VMEM((2, 128, PW), F32)],
        compiler_params=pltpu.CompilerParams(vmem_limit_bytes=16 * MIB),
        cost_estimate=pl.CostEstimate(flops=40_000_000, bytes_accessed=60_000_000, transcendentals=0),
        name="factor",
    )(t)


def offer_kernel(matrix_ref, pick_ref, out_ref):
    matrix = matrix_ref[...]
    offer = dot_nt(matrix, pick_ref[...])
    for i in range(PROW):
        out_ref[i, :, :PW] = offer
        out_ref[i, :, PW:] = matrix[:, :PW]


def offered(matrix, pick):
    return pl.pallas_call(
        offer_kernel,
        out_shape=jax.ShapeDtypeStruct((PROW, NB, 2 * PW), F32),
        in_specs=[VMEM] * 2,
        out_specs=VMEM,
        compiler_params=pltpu.CompilerParams(vmem_limit_bytes=16 * MIB),
        name="offer",
    )(matrix, pick)


def finish_kernel(pivot_ref, matrix_ref, offers_ref, panel_ref, packed_ref, loinv_ref, upinv_ref, out_ref, low_ref):
    row_group = lax.axis_index(AY)
    col_group = lax.axis_index(AX) * NZ + lax.axis_index(AZ)
    rows = lax.broadcasted_iota(jnp.int32, (PW, ROWS_DEV), 1) + row_group * ROWS_DEV
    pick = jnp.where(pivot_ref[...] == rows, 1.0, 0.0)
    hit = jnp.sum(pick, axis=0, keepdims=True) > 0.0
    low_ref[...] = dotf(loinv_ref[...], panel_ref[...])
    matrix = jnp.where(hit, dotf(offers_ref[0, :, PW:], pick), matrix_ref[...])
    inc = offers_ref[0, :, :PW]
    for i in range(1, PROW):
        inc = inc + offers_ref[i, :, :PW]
    upper = dotf(inc, upinv_ref[...])
    out_ref[...] = matrix - dotf(upper, low_ref[...])

    @pl.when(row_group == 0)
    def _():
        out_ref[:, :PW] = upper

    @pl.when(col_group < OWNERS)
    def _():
        at = pl.ds(pl.multiple_of(col_group * NB, NB), NB)
        out_ref[...] = low_ref[at, :]

        @pl.when(row_group == 0)
        def _():
            out_ref[:, :PW] = packed_ref[at, :]


def finish(pivot, matrix, offers, panel, packed, loinv, upinv):
    return pl.pallas_call(
        finish_kernel,
        out_shape=jax.ShapeDtypeStruct((NB, ROWS_DEV), F32),
        in_specs=[VMEM] * 7,
        out_specs=VMEM,
        scratch_shapes=[pltpu.VMEM((PW, ROWS_DEV), F32)],
        compiler_params=pltpu.CompilerParams(vmem_limit_bytes=16 * MIB),
        name="finish",
    )(pivot, matrix, offers, panel, packed, loinv, upinv)


def per_device(matrix_slab, contributions, target_column, target_rows, live_rows, pivot_index):
    row_group = lax.axis_index(AY)
    pan, dense = scatter(target_column, target_rows, live_rows, contributions[0], matrix_slab)
    pivot = pivot_index[0]
    pick = (pivot[:, None] == row_group * ROWS_DEV + jnp.arange(ROWS_DEV)[None, :]).astype(F32)
    hit = jnp.sum(pick, axis=0) > 0

    along_z = ring_sum_halves(dense[:4] + [None] + dense[6:], dense[4:6], AZ, NZ)
    pair = next(along_z)
    chunk = exchange(pan, AX).sum(axis=0).reshape(NZ, NB // NZ, ROWS_DEV)
    chunk, pair = tied(chunk, pair)
    pair = along_z.send(pair)
    chunk = exchange(chunk, AZ).sum(axis=0)
    offer = jnp.concatenate([dot_nt(chunk, pick), chunk[:, :PW]], axis=1)
    offers, pair = tied(copied(offer, PROW), pair)
    pair = along_z.send(pair)
    offers = exchange(offers, AY)
    moved = offers[0, :, PW:]
    chunk = jnp.where(hit[None, :], dotf(moved, pick), chunk)
    both = jnp.concatenate([offers[:, :, :PW].sum(axis=0), chunk], axis=1)
    both = exchange(copied(both, NZ), AZ).reshape(NB, PW + ROWS_DEV)
    both, pair = tied(both, pair)
    pair = along_z.send(pair)
    both, pair = tied(copied(both, NX), pair)
    along_x = ring_sum(along_z.send(pair), AX, NX)
    pair = next(along_x)
    both, pair = tied(exchange(both, AX).reshape(PW, PW + ROWS_DEV), pair)
    pair = along_x.send(pair)
    matrix = matrix_slab + along_x.send(pair)
    with jax.named_scope("slab_swap"):
        offer = offered(matrix, pick)
        diag = lax.optimization_barrier((both[:, :PW], offer))[0]
        offers = exchange(offer, AY)
    packed, loinv, upinv = factor(diag)
    return finish(pivot[:, None], matrix, offers, both[:, PW:], packed, loinv, upinv)


def solution(mesh):
    torus = Mesh(mesh.devices.reshape(mesh.shape["prow"], NX, NZ), (AY, AX, AZ))
    placed = (
        P(PCOL, AY),
        P(AY, PCOL, None, None),
        P(AY, PCOL),
        P(AY, PCOL),
        P(AY, PCOL),
        P(),
    )
    return jax.shard_map(
        per_device, mesh=torus, in_specs=placed, out_specs=P(PCOL, AY), check_vma=False
    )
```
